512 devices in a mesh: ctx: 8 (over x, core), hs: 64 (over z, y).
Axes of the slice: x: 4, y: 8, z: 8, core: 2. Of those that a mesh axis runs over, the one named last changes fastest.
Arguments:
- key_rows: bfloat16 [64, 4096, 512], P('hs', 'ctx'), may hold values from -6 to 6
- value_rows: bfloat16 [64, 4096, 512], P('hs', 'ctx'), may hold values from -6 to 6
- query_rows: bfloat16 [64, 4096, 512], P('hs', 'ctx'), may hold values from -6 to 6
- step_rates: float32 [64, 4096], P('hs', 'ctx'), may hold values from 0.0003 to 0.003
- fast_gate: bfloat16 [64, 512, 512], P('hs', 'ctx'), may hold values from -0.25 to 0.25
- fast_up: bfloat16 [64, 512, 512], P('hs', 'ctx'), may hold values from -0.25 to 0.25
- fast_down: bfloat16 [64, 512, 512], P('hs', 'ctx'), may hold values from -0.25 to 0.25
- out_gain: float32 [2048], replicated, may hold values from 0.1 to 1.9
- gate_input: bfloat16 [4096, 16, 2048], P(('ctx', 'hs')), may hold values from -6 to 6
- out_weight: bfloat16 [2048, 1024], P('hs'), may hold values from -0.125 to 0.125
Outputs:
- layer_out: bfloat16 [4096, 16, 1024], P(('ctx', 'hs'))
The draws below stay inside these ranges and needn't reach their ends.
All inputs are finite; a program needn't handle non-finite values.
Results may differ from the reference program's by a relative error of at most 0.01.
Values may be sent and summed in bfloat16 or wider, within the bound.
No kernel may reach another device: no remote copies, remote signals or barrier semaphores. Data moves between devices by JAX's collectives and lax.ppermute only.
A program may use at most 64 MiB of HBM per device.

```python
import math
import jax
import jax.numpy as jnp
from jax import lax

D = 2048
HEADS = 4
DH = 512
FH = 512
DOUT = 1024
GROUP = 4096
SEQS = 16
PAIRS = 64


def level_of(own_key, shape, shards, low, largest):
    gain, own = 1.0, jax.random.fold_in(own_key, 6)
    for position, blocks in shards:
        draws = jnp.exp(jax.random.uniform(jax.random.fold_in(own, position), (blocks,), jnp.float32, low / len(shards), largest / len(shards)))
        gain = gain * jnp.repeat(draws, shape[position] // blocks).reshape([-1 if axis == position else 1 for axis in range(len(shape))])
    return gain


def centred(key, extent, scale, limit, pieces=(), dtype=jnp.bfloat16):
    drawn = jax.random.normal(key, extent, jnp.float32) * scale
    if len(pieces) > 0:
        drawn = level_of(key, extent, pieces, -0.22, 0.18) * drawn
    return jnp.clip(drawn, min=-limit, max=limit).astype(dtype)


def setup_inputs(seed: int = 0) -> dict:
    arg_keys = jax.random.split(jax.random.key(seed), 11)
    key_rows = centred(arg_keys[0], (PAIRS, GROUP, DH), 1.0, 6.0, ((0, 64), (1, 8)))
    value_rows = centred(arg_keys[1], (PAIRS, GROUP, DH), 1.0, 6.0, ((0, 64), (1, 8)))
    query_rows = centred(arg_keys[2], (PAIRS, GROUP, DH), 1.0, 6.0, ((0, 64), (1, 8)))
    step_rates = jnp.clip(jnp.exp(math.log(0.003) - 2.3025851 * jax.random.uniform(arg_keys[3], (PAIRS, GROUP), jnp.float32) ** level_of(arg_keys[3], (PAIRS, GROUP), ((0, 64), (1, 8)), -0.2, 0.2)), 0.0003, 0.003)
    fast_gate = centred(arg_keys[4], (PAIRS, FH, DH), DH ** -0.5, 0.25, ((0, 64), (1, 8)))
    fast_up = centred(arg_keys[5], (PAIRS, FH, DH), DH ** -0.5, 0.25, ((0, 64), (1, 8)))
    fast_down = centred(arg_keys[6], (PAIRS, DH, FH), FH ** -0.5, 0.25, ((0, 64), (1, 8)))
    out_gain = jnp.clip(1.0 + 0.18 * jax.random.normal(arg_keys[7], (D,), jnp.float32), 0.1, 1.9)
    gate_input = centred(arg_keys[8], (GROUP, SEQS, D), 1.0, 6.0, ((0, 512),))
    out_weight = centred(arg_keys[9], (D, DOUT), D ** -0.5, 0.125, ((0, 64),))
    return dict(key_rows=key_rows, value_rows=value_rows, query_rows=query_rows, step_rates=step_rates, fast_gate=fast_gate, fast_up=fast_up, fast_down=fast_down, out_gain=out_gain, gate_input=gate_input, out_weight=out_weight)


epsilon = 1e-06

def rescale_rows(weight, update):
    base = weight.astype(jnp.float32)
    moved = base + update
    factor = jnp.sqrt(lax.optimization_barrier(jnp.mean(base * base, -1, keepdims=True)) + epsilon) / jnp.sqrt(lax.optimization_barrier(jnp.mean(moved * moved, -1, keepdims=True)) + epsilon)
    return (moved * factor).astype(jnp.bfloat16)

def inner_rows(left, right):
    return lax.dot_general(left, right, (((0,), (0,)), ((), ())), preferred_element_type=jnp.float32)

def one_pair(packed):
    key_row, value_row, query_row, rate_row, gate_fast, up_fast, down_fast = packed
    pre_gate = jnp.dot(key_row, gate_fast.T, preferred_element_type=jnp.float32)
    pre_up = jnp.dot(key_row, up_fast.T, preferred_element_type=jnp.float32)
    sig_gate = jax.nn.sigmoid(pre_gate)
    act_gate = pre_gate * sig_gate
    hidden = (act_gate * pre_up).astype(jnp.bfloat16)
    scaled = (rate_row[:, None] * value_row.astype(jnp.float32)).astype(jnp.bfloat16)
    grad_down = inner_rows(scaled, hidden)
    back_hidden = jnp.dot(scaled, down_fast, preferred_element_type=jnp.float32)
    back_gate = (back_hidden * pre_up * sig_gate * (1.0 + pre_gate * (1.0 - sig_gate))).astype(jnp.bfloat16)
    back_up = (back_hidden * act_gate).astype(jnp.bfloat16)
    grad_gate = inner_rows(back_gate, key_row)
    grad_up = inner_rows(back_up, key_row)
    new_gate = rescale_rows(gate_fast, grad_gate)
    new_up = rescale_rows(up_fast, grad_up)
    new_down = rescale_rows(down_fast, grad_down)
    query_gate = jnp.dot(query_row, new_gate.T, preferred_element_type=jnp.float32)
    query_up = jnp.dot(query_row, new_up.T, preferred_element_type=jnp.float32)
    query_hidden = (jax.nn.silu(query_gate) * query_up).astype(jnp.bfloat16)
    return jnp.dot(query_hidden, new_down.T, preferred_element_type=jnp.float32).astype(jnp.bfloat16)

def reference(key_rows, value_rows, query_rows, step_rates, fast_gate, fast_up, fast_down, out_gain, gate_input, out_weight):
    head_out = lax.map(one_pair, (key_rows, value_rows, query_rows, step_rates, fast_gate, fast_up, fast_down))
    mixed = head_out.reshape(SEQS, HEADS, GROUP, DH).transpose(2, 0, 1, 3).astype(jnp.float32)
    square = lax.optimization_barrier(jnp.mean(mixed * mixed, -1, keepdims=True))
    scaled_heads = mixed * lax.rsqrt(square + epsilon) * out_gain.reshape(HEADS, DH)
    normed = (scaled_heads.reshape(GROUP, SEQS, D) * jax.nn.silu(gate_input.astype(jnp.float32))).astype(jnp.bfloat16)
    result = jnp.dot(normed.reshape(GROUP * SEQS, D), out_weight, preferred_element_type=jnp.float32)
    return result.astype(jnp.bfloat16).reshape(GROUP, SEQS, DOUT)
```

```python
import functools

import jax
import jax.numpy as jnp
from jax import lax
from jax.experimental import pallas as pl
from jax.experimental.pallas import tpu as pltpu
from jax.sharding import Mesh
from jax.sharding import PartitionSpec as P

epsilon = 1e-06
BF = jnp.bfloat16
F32 = jnp.float32
VMEM = pl.BlockSpec(memory_space=pltpu.VMEM)
SMEM = pl.BlockSpec(memory_space=pltpu.SMEM)
PARAMS = pltpu.CompilerParams(vmem_limit_bytes=40 * 1024 * 1024)


def dot(left, right, a, b):
    return lax.dot_general(left, right, (((a,), (b,)), ((), ())), preferred_element_type=F32)


def assemble(core, own, other, fulls):
    chips, rows, _ = own.shape
    part = rows // 3
    for i, full in enumerate(fulls):
        for x in range(chips):
            mine = pl.multiple_of(x * 2 * part + core * part, part)
            theirs = pl.multiple_of(x * 2 * part + (1 - core) * part, part)
            full[pl.ds(mine, part), :] = own[x, i * part : (i + 1) * part, :]
            full[pl.ds(theirs, part), :] = other[x, i * part : (i + 1) * part, :]


def grad_kernel(core_ref, key, value, rate, own, other, keep, send, gate, up, down, g0, g1, g2):
    core = core_ref[0]
    assemble(core, own, other, (gate, up, down))
    tokens, width = key.shape
    column = jnp.transpose(jnp.broadcast_to(rate[...], (128, tokens)))
    scaled = (jnp.concatenate([column] * (width // 128), axis=1) * value[...].astype(F32)).astype(BF)
    k = key[...]
    units = gate.shape[0]
    step = 256
    for n in range(0, units, step):
        pre_gate = dot(k, gate[n : n + step, :], 1, 1)
        pre_up = dot(k, up[n : n + step, :], 1, 1)
        back = dot(scaled, down[:, n : n + step], 1, 0)
        sig = jax.nn.sigmoid(pre_gate)
        act = pre_gate * sig
        hidden = (act * pre_up).astype(BF)
        back_gate = (back * pre_up * sig * (1.0 + pre_gate * (1.0 - sig))).astype(BF)
        back_up = (back * act).astype(BF)
        g0[n : n + step, :] = dot(back_gate, k, 0, 0).astype(BF)
        g1[n : n + step, :] = dot(back_up, k, 0, 0).astype(BF)
        g2[:, n : n + step] = dot(scaled, hidden, 0, 0).astype(BF)
    chips, rows, _ = keep.shape
    part = rows // 3
    for i, grad in enumerate((g0, g1, g2)):
        for x in range(chips):
            mine = pl.multiple_of(x * 2 * part + core * part, part)
            theirs = pl.multiple_of(x * 2 * part + (1 - core) * part, part)
            keep[x, i * part : (i + 1) * part, :] = grad[pl.ds(mine, part), :]
            send[x, i * part : (i + 1) * part, :] = grad[pl.ds(theirs, part), :]


def rescale_kernel(parts, weight, new):
    base = weight[...].astype(F32)
    moved = base
    total = parts[0].astype(F32)
    for x in range(1, parts.shape[0]):
        total = total + parts[x].astype(F32)
    moved = base + total
    factor = jnp.sqrt(jnp.mean(base * base, -1, keepdims=True) + epsilon) / jnp.sqrt(
        jnp.mean(moved * moved, -1, keepdims=True) + epsilon
    )
    new[...] = (moved * factor).astype(BF)


def query_kernel(core_ref, query, own, other, out, gate, up, down):
    assemble(core_ref[0], own, other, (gate, up, down))
    q = query[...]
    units = gate.shape[0]
    step = 256
    pieces = []
    for n in range(0, units, step):
        pre_gate = dot(q, gate[n : n + step, :], 1, 1)
        pre_up = dot(q, up[n : n + step, :], 1, 1)
        pieces.append((pre_gate * jax.nn.sigmoid(pre_gate) * pre_up).astype(BF))
    hidden = jnp.concatenate(pieces, axis=1)
    out[...] = dot(hidden, down[...], 1, 1).astype(BF)


def output_kernel(moved, gain, gate, weight, out, *, seqs, heads):
    total, size = moved.shape
    rows = total // heads
    tokens = rows // seqs
    everything = moved[...]
    row = lax.broadcasted_iota(jnp.int32, (rows, total), 0)
    column = lax.broadcasted_iota(jnp.int32, (rows, total), 1)
    acc = None
    for h in range(heads):
        source = (row % seqs * heads + h) * tokens + row // seqs
        pick = jnp.where(column == source, 1.0, 0.0).astype(BF)
        mixed = dot(pick, everything, 1, 0)
        square = jnp.mean(mixed * mixed, -1, keepdims=True)
        g = gate[:, h * size : (h + 1) * size].astype(F32)
        normed = mixed * lax.rsqrt(square + epsilon) * gain[:, h * size : (h + 1) * size] * (
            g * jax.nn.sigmoid(g)
        )
        part = dot(normed.astype(BF), weight[h * size : (h + 1) * size, :], 1, 0)
        acc = part if acc is None else acc + part
    out[...] = acc.astype(BF)


def swap(a):
    return lax.ppermute(a, "core", [(0, 1), (1, 0)])


def body(
    key_rows,
    value_rows,
    query_rows,
    step_rates,
    fast_gate,
    fast_up,
    fast_down,
    out_gain,
    gate_input,
    out_weight,
):
    chips = lax.axis_size("x")
    core = lax.axis_index("core").astype(jnp.int32).reshape(1)
    tokens, width = key_rows.shape[1:]
    part = fast_gate.shape[1]
    units = part * chips * 2
    full_weight = lax.all_gather(out_weight, "hs", axis=0, tiled=True)
    weights = jnp.concatenate([fast_gate[0], fast_up[0], fast_down[0]], axis=0)
    rows = weights.shape[0]
    own = lax.all_gather(weights, "x", axis=0, tiled=False)
    other = swap(own)
    piece = jax.ShapeDtypeStruct((chips, rows, width), BF)
    square = pltpu.VMEM((units, width), BF)
    keep, send = pl.pallas_call(
        grad_kernel,
        out_shape=(piece, piece),
        in_specs=[SMEM] + [VMEM] * 5,
        out_specs=(VMEM, VMEM),
        scratch_shapes=[square] * 6,
        compiler_params=PARAMS,
        name="grads",
    )(core, key_rows[0], value_rows[0], step_rates, own, other)
    summed = (keep.astype(F32) + swap(send).astype(F32)).astype(BF)
    parts = lax.all_to_all(summed, "x", split_axis=0, concat_axis=0, tiled=True)
    new = pl.pallas_call(
        rescale_kernel,
        out_shape=jax.ShapeDtypeStruct((rows, width), BF),
        in_specs=[VMEM] * 2,
        out_specs=VMEM,
        compiler_params=PARAMS,
        name="rescale",
    )(parts, weights)
    own = lax.all_gather(new, "x", axis=0, tiled=False)
    other = swap(own)
    head_out = pl.pallas_call(
        query_kernel,
        out_shape=jax.ShapeDtypeStruct((tokens, width), BF),
        in_specs=[SMEM] + [VMEM] * 3,
        out_specs=VMEM,
        scratch_shapes=[square] * 3,
        compiler_params=PARAMS,
        name="query",
    )(core, query_rows[0], own, other)
    pairs = lax.axis_size("hs")
    blocks = head_out.reshape(pairs, tokens // pairs, width)
    moved = lax.all_to_all(blocks, "hs", split_axis=0, concat_axis=0, tiled=True)
    few, seqs, model = gate_input.shape
    heads = model // width
    columns = out_weight.shape[1]
    result = pl.pallas_call(
        functools.partial(output_kernel, seqs=seqs, heads=heads),
        out_shape=jax.ShapeDtypeStruct((few * seqs, columns), BF),
        in_specs=[VMEM] * 4,
        out_specs=VMEM,
        compiler_params=PARAMS,
        name="project",
    )(
        moved.reshape(tokens, width),
        out_gain.reshape(1, model),
        gate_input.reshape(few * seqs, model),
        full_weight,
    )
    return result.reshape(few, seqs, columns)


def solution(mesh):
    ctx, pairs = mesh.devices.shape
    split = Mesh(mesh.devices.reshape(ctx // 2, 2, pairs), ("x", "core", "hs"))
    c = ("x", "core")
    return jax.shard_map(
        body,
        mesh=split,
        in_specs=(
            P("hs", c, None),
            P("hs", c, None),
            P("hs", c, None),
            P("hs", c),
            P("hs", c, None),
            P("hs", c, None),
            P("hs", c, None),
            P(),
            P(c + ("hs",), None, None),
            P("hs", None),
        ),
        out_specs=P(c + ("hs",), None, None),
        check_vma=False,
    )
```

```python
import functools

import jax
import jax.numpy as jnp
from jax import lax
from jax.experimental import pallas as pl
from jax.experimental.pallas import tpu as pltpu
from jax.sharding import Mesh
from jax.sharding import PartitionSpec as P

epsilon = 1e-06
BF = jnp.bfloat16
F32 = jnp.float32
VMEM = pl.BlockSpec(memory_space=pltpu.VMEM)
SMEM = pl.BlockSpec(memory_space=pltpu.SMEM)
PARAMS = pltpu.CompilerParams(vmem_limit_bytes=24 * 1024 * 1024)


def dot(left, right, a, b):
    return lax.dot_general(left, right, (((a,), (b,)), ((), ())), preferred_element_type=F32)


def assemble(core, own, other, fulls):
    chips, rows, _ = own.shape
    part = rows // 3
    for i, full in enumerate(fulls):
        for x in range(chips):
            mine = pl.multiple_of(x * 2 * part + core * part, part)
            theirs = pl.multiple_of(x * 2 * part + (1 - core) * part, part)
            full[pl.ds(mine, part), :] = own[x, i * part : (i + 1) * part, :]
            full[pl.ds(theirs, part), :] = other[x, i * part : (i + 1) * part, :]


def grad_kernel(core_ref, key, value, rate, own, other, keep, send, gate, up, down, g0, g1, g2):
    core = core_ref[0]
    assemble(core, own, other, (gate, up, down))
    tokens, width = key.shape
    column = jnp.transpose(jnp.broadcast_to(rate[...], (128, tokens)))
    scaled = (jnp.concatenate([column] * (width // 128), axis=1) * value[...].astype(F32)).astype(BF)
    k = key[...]
    units = gate.shape[0]
    step = 256
    for n in range(0, units, step):
        pre_gate = dot(k, gate[n : n + step, :], 1, 1)
        pre_up = dot(k, up[n : n + step, :], 1, 1)
        back = dot(scaled, down[:, n : n + step], 1, 0)
        sig = jax.nn.sigmoid(pre_gate)
        act = pre_gate * sig
        hidden = (act * pre_up).astype(BF)
        back_gate = (back * pre_up * sig * (1.0 + pre_gate * (1.0 - sig))).astype(BF)
        back_up = (back * act).astype(BF)
        g0[n : n + step, :] = dot(back_gate, k, 0, 0).astype(BF)
        g1[n : n + step, :] = dot(back_up, k, 0, 0).astype(BF)
        g2[:, n : n + step] = dot(scaled, hidden, 0, 0).astype(BF)
    chips, rows, _ = keep.shape
    part = rows // 3
    for i, grad in enumerate((g0, g1, g2)):
        for x in range(chips):
            base = lax.rem(core_ref[1] + x, chips) * 2 * part
            mine = pl.multiple_of(base + core * part, part)
            theirs = pl.multiple_of(base + (1 - core) * part, part)
            keep[x, i * part : (i + 1) * part, :] = grad[pl.ds(mine, part), :]
            send[x, i * part : (i + 1) * part, :] = grad[pl.ds(theirs, part), :]


def rescale_kernel(p0, p1, p2, p3, weight, new):
    base = weight[...].astype(F32)
    total = p0[...].astype(F32) + p1[...].astype(F32)
    moved = base + (total + (p2[...].astype(F32) + p3[...].astype(F32)))
    factor = jnp.sqrt(jnp.mean(base * base, -1, keepdims=True) + epsilon) / jnp.sqrt(
        jnp.mean(moved * moved, -1, keepdims=True) + epsilon
    )
    new[...] = (moved * factor).astype(BF)


def query_kernel(core_ref, query, own, other, out, gate, up, down):
    assemble(core_ref[0], own, other, (gate, up, down))
    q = query[...]
    units = gate.shape[0]
    step = 256
    pieces = []
    for n in range(0, units, step):
        pre_gate = dot(q, gate[n : n + step, :], 1, 1)
        pre_up = dot(q, up[n : n + step, :], 1, 1)
        pieces.append((pre_gate * jax.nn.sigmoid(pre_gate) * pre_up).astype(BF))
    hidden = jnp.concatenate(pieces, axis=1)
    out[...] = dot(hidden, down[...], 1, 1).astype(BF)


def output_kernel(core_ref, moved, gain, gate, mine, theirs, out, *, seqs, heads):
    total, size = moved.shape
    rows = total // heads
    tokens = rows // seqs
    row = lax.broadcasted_iota(jnp.int32, (rows, total), 0)
    column = lax.broadcasted_iota(jnp.int32, (rows, total), 1)
    first = (row % seqs * heads) * tokens + row // seqs
    left = right = None
    for h in range(heads):
        pick = jnp.where(column == first + h * tokens, 1.0, 0.0).astype(BF)
        mixed = dot(pick, moved[...], 1, 0)
        square = jnp.mean(mixed * mixed, -1, keepdims=True)
        span = slice(h * size, (h + 1) * size)
        g = gate[:, span].astype(F32)
        normed = mixed * lax.rsqrt(square + epsilon) * gain[:, span] * (g * jax.nn.sigmoid(g))
        normed = normed.astype(BF)
        one, two = dot(normed, mine[span, :], 1, 0), dot(normed, theirs[span, :], 1, 0)
        left = one if left is None else left + one
        right = two if right is None else right + two
    half = mine.shape[1]
    core = core_ref[0]
    out[:, pl.ds(pl.multiple_of(core * half, half), half)] = left.astype(BF)
    out[:, pl.ds(pl.multiple_of((1 - core) * half, half), half)] = right.astype(BF)


def swap(a):
    return lax.ppermute(a, "core", [(0, 1), (1, 0)])


def body(
    key_rows,
    value_rows,
    query_rows,
    step_rates,
    fast_gate,
    fast_up,
    fast_down,
    out_gain,
    gate_input,
    out_weight,
):
    chips = lax.axis_size("x")
    core = jnp.stack([lax.axis_index(a).astype(jnp.int32) for a in ("core", "x")])
    tokens, width = key_rows.shape[1:]
    part = fast_gate.shape[1]
    units = part * chips * 2
    count = lax.axis_size("hs")
    depth, half = out_weight.shape[0], out_weight.shape[1] // 2
    piece = lax.dynamic_slice_in_dim(out_weight, core[0] * half, half, 1)
    mine = lax.all_to_all(
        jnp.broadcast_to(piece, (count, depth, half)), "hs", split_axis=0, concat_axis=0, tiled=True
    ).reshape(count * depth, half)
    weights = jnp.concatenate([fast_gate[0], fast_up[0], fast_down[0]], axis=0)
    rows = weights.shape[0]
    own = lax.all_gather(weights, "x", axis=0, tiled=False)
    other = swap(own)
    piece = jax.ShapeDtypeStruct((chips, rows, width), BF)
    square = pltpu.VMEM((units, width), BF)
    keep, send = pl.pallas_call(
        grad_kernel,
        out_shape=(piece, piece),
        in_specs=[SMEM] + [VMEM] * 5,
        out_specs=(VMEM, VMEM),
        scratch_shapes=[square] * 6,
        compiler_params=PARAMS,
        name="grads",
    )(core, key_rows[0], value_rows[0], step_rates, own, other)
    got = swap(send)
    parts = []
    for r in range(chips):
        summed = (keep[r].astype(F32) + got[r].astype(F32)).astype(BF)
        ring = [(x, (x + r) % chips) for x in range(chips)]
        parts.append(lax.ppermute(summed, "x", ring) if r else summed)
    new = pl.pallas_call(
        rescale_kernel,
        out_shape=jax.ShapeDtypeStruct((rows, width), BF),
        in_specs=[VMEM] * 5,
        out_specs=VMEM,
        compiler_params=PARAMS,
        name="rescale",
    )(*parts, weights)
    own = lax.all_gather(new, "x", axis=0, tiled=False)
    other = swap(own)
    head_out = pl.pallas_call(
        query_kernel,
        out_shape=jax.ShapeDtypeStruct((tokens, width), BF),
        in_specs=[SMEM] + [VMEM] * 3,
        out_specs=VMEM,
        scratch_shapes=[square] * 3,
        compiler_params=PARAMS,
        name="query",
    )(core, query_rows[0], own, other)
    theirs = swap(mine)
    pairs = lax.axis_size("hs")
    blocks = head_out.reshape(pairs, tokens // pairs, width)
    moved = lax.all_to_all(blocks, "hs", split_axis=0, concat_axis=0, tiled=True)
    few, seqs, model = gate_input.shape
    heads = model // width
    columns = out_weight.shape[1]
    result = pl.pallas_call(
        functools.partial(output_kernel, seqs=seqs, heads=heads),
        out_shape=jax.ShapeDtypeStruct((few * seqs, columns), BF),
        in_specs=[SMEM] + [VMEM] * 5,
        out_specs=VMEM,
        compiler_params=PARAMS,
        name="project",
    )(
        core,
        moved.reshape(tokens, width),
        out_gain.reshape(1, model),
        gate_input.reshape(few * seqs, model),
        mine,
        theirs,
    )
    return result.reshape(few, seqs, columns)


def solution(mesh):
    ctx, pairs = mesh.devices.shape
    split = Mesh(mesh.devices.reshape(ctx // 2, 2, pairs), ("x", "core", "hs"))
    c = ("x", "core")
    return jax.shard_map(
        body,
        mesh=split,
        in_specs=(
            P("hs", c, None),
            P("hs", c, None),
            P("hs", c, None),
            P("hs", c),
            P("hs", c, None),
            P("hs", c, None),
            P("hs", c, None),
            P(),
            P(c + ("hs",), None, None),
            P("hs", None),
        ),
        out_specs=P(c + ("hs",), None, None),
        check_vma=False,
    )
```

```python
import functools

import jax
import jax.numpy as jnp
from jax import lax
from jax.experimental import pallas as pl
from jax.experimental.pallas import tpu as pltpu
from jax.sharding import Mesh
from jax.sharding import PartitionSpec as P

epsilon = 1e-06
BF = jnp.bfloat16
F32 = jnp.float32
VMEM = pl.BlockSpec(memory_space=pltpu.VMEM)
SMEM = pl.BlockSpec(memory_space=pltpu.SMEM)
PARAMS = pltpu.CompilerParams(vmem_limit_bytes=16 * 1024 * 1024)


def dot(left, right, a, b):
    return lax.dot_general(left, right, (((a,), (b,)), ((), ())), preferred_element_type=F32)


def pack_kernel(key, value, rate, down, out):
    tokens, width = key.shape
    column = jnp.transpose(jnp.broadcast_to(rate[...], (128, tokens)))
    out[:tokens, :] = key[...]
    out[tokens : 2 * tokens, :] = (
        jnp.concatenate([column] * (width // 128), axis=1) * value[...].astype(F32)
    ).astype(BF)
    out[2 * tokens :, :] = down[...]


def choose_kernel(place_ref, gate, up, down, other, out):
    core = place_ref[0]
    part, width = gate.shape
    half = width // 2
    own, theirs = down[...], other[other.shape[0] - part :, :]
    first = core == 0
    rows = jnp.concatenate(
        [jnp.where(first, own.astype(F32), theirs.astype(F32)), jnp.where(first, theirs.astype(F32), own.astype(F32))],
        axis=0,
    )
    unit = lax.broadcasted_iota(jnp.int32, (width, half), 0)
    slot = lax.broadcasted_iota(jnp.int32, (width, half), 1)
    source = (slot // part * 2 + core) * part + slot % part
    chosen = dot(rows.astype(BF), jnp.where(unit == source, 1.0, 0.0).astype(BF), 1, 0).astype(BF)
    out[:part, :] = gate[...]
    out[part : 2 * part, :] = up[...]
    out[2 * part : 3 * part, :half] = chosen[:part, :]
    out[2 * part : 3 * part, half:] = chosen[part:, :]
    total = jnp.sum(rows * rows, -1, keepdims=True)
    total = jnp.transpose(jnp.broadcast_to(total, (2 * part, 128)))[:1, :]
    high = total.astype(BF).astype(F32)
    middle = (total - high).astype(BF).astype(F32)
    low = total - high - middle
    tail = out.shape[0] - 3 * part
    row = lax.broadcasted_iota(jnp.int32, (tail, 2 * part), 0)
    terms = jnp.where(row == 0, high, jnp.where(row == 1, middle, jnp.where(row == 2, low, 0.0)))
    out[3 * part :, :] = jnp.concatenate(
        [terms, jnp.zeros((tail, width - 2 * part), F32)], axis=1
    ).astype(BF)


def halves(held):
    chips, _, width = held.shape
    part = width // (2 * chips)
    half = width // 2
    gate = jnp.concatenate([held[x, :part, :] for x in range(chips)], axis=0)
    up = jnp.concatenate([held[x, part : 2 * part, :] for x in range(chips)], axis=0)
    down = jnp.concatenate(
        [
            held[x, 2 * part : 3 * part, c * half : (c + 1) * half]
            for x in range(chips)
            for c in range(2)
        ],
        axis=0,
    )
    return gate, up, down


def grad_kernel(place_ref, mine, theirs, held, o0, o1, o2, o3, g0, g1, g2):
    gate, up, down = halves(held)
    chips, _, width = held.shape
    part = width // (2 * chips)
    half = width // 2
    tokens = width
    total = None
    for rows in (mine, theirs):
        k, scaled = rows[:tokens, :], rows[tokens : 2 * tokens, :]
        pre_gate = dot(k, gate, 1, 1)
        pre_up = dot(k, up, 1, 1)
        back = dot(scaled, down, 1, 0)
        sig = jax.nn.sigmoid(pre_gate)
        act = pre_gate * sig
        hidden = (act * pre_up).astype(BF)
        back_gate = (back * pre_up * sig * (1.0 + pre_gate * (1.0 - sig))).astype(BF)
        back_up = (back * act).astype(BF)
        grads = (dot(back_gate, k, 0, 0), dot(back_up, k, 0, 0), dot(scaled, hidden, 0, 0))
        if total is None:
            g0[...], g1[...], g2[...] = grads
            total = grads
        else:
            for g, grad in zip((g0, g1, g2), grads):
                g[...] += grad
    for r, out in enumerate((o0, o1, o2, o3)):
        x = lax.rem(place_ref[1] + r, chips)
        spot = pl.multiple_of(x * part, part)
        out[:part, :] = g0[pl.ds(spot, part), :].astype(BF)
        out[part : 2 * part, :] = g1[pl.ds(spot, part), :].astype(BF)
        for c in range(2):
            spot = pl.multiple_of((2 * x + c) * part, part)
            out[2 * part :, c * half : (c + 1) * half] = g2[pl.ds(spot, part), :].astype(BF)


def rescale_kernel(p0, p1, p2, p3, weight, new):
    rows = p0.shape[0]
    whole = rows // 3 * 2
    base = weight[:rows, :].astype(F32)
    total = p0[...].astype(F32) + p1[...].astype(F32)
    moved = base + (total + (p2[...].astype(F32) + p3[...].astype(F32)))
    factor = jnp.sqrt(jnp.mean(base * base, -1, keepdims=True) + epsilon) / jnp.sqrt(
        jnp.mean(moved * moved, -1, keepdims=True) + epsilon
    )
    new[:whole, :] = (moved * factor)[:whole, :].astype(BF)
    new[whole:, :] = moved[whole:, :].astype(BF)


def query_kernel(query, held, own, other, out):
    chips, _, width = own.shape
    q = query[...]
    result = squares = None
    for rows in (own, other):
        gate, up, down = halves(rows)
        pre_gate = dot(q, gate, 1, 1)
        pre_up = dot(q, up, 1, 1)
        hidden = (pre_gate * jax.nn.sigmoid(pre_gate) * pre_up).astype(BF)
        part = dot(hidden, down, 1, 1)
        d = down.astype(F32)
        square = jnp.sum(d * d, -1, keepdims=True)
        result = part if result is None else result + part
        squares = square if squares is None else squares + square
    moved = jnp.transpose(jnp.broadcast_to(squares, (width, 128)))[:1, :]
    span = width // chips
    tail = own.shape[1]
    base = jnp.concatenate(
        [
            jnp.sum(held[x, tail:, :span].astype(F32), 0, keepdims=True)
            for x in range(chips)
        ],
        axis=1,
    )
    factor = jnp.sqrt(base * (1.0 / width) + epsilon) / jnp.sqrt(moved * (1.0 / width) + epsilon)
    out[...] = (result * factor).astype(BF)


def output_kernel(core_ref, moved, gain, gate, mine, theirs, out, *, seqs, heads):
    total, size = moved.shape
    rows = total // heads
    tokens = rows // seqs
    row = lax.broadcasted_iota(jnp.int32, (rows, total), 0)
    column = lax.broadcasted_iota(jnp.int32, (rows, total), 1)
    first = (row % seqs * heads) * tokens + row // seqs
    left = right = None
    for h in range(heads):
        pick = jnp.where(column == first + h * tokens, 1.0, 0.0).astype(BF)
        mixed = dot(pick, moved[...], 1, 0)
        square = jnp.mean(mixed * mixed, -1, keepdims=True)
        span = slice(h * size, (h + 1) * size)
        g = gate[:, span].astype(F32)
        normed = mixed * lax.rsqrt(square + epsilon) * gain[:, span] * (g * jax.nn.sigmoid(g))
        normed = normed.astype(BF)
        one, two = dot(normed, mine[span, :], 1, 0), dot(normed, theirs[span, :], 1, 0)
        left = one if left is None else left + one
        right = two if right is None else right + two
    half = mine.shape[1]
    core = core_ref[0]
    out[:, pl.ds(pl.multiple_of(core * half, half), half)] = left.astype(BF)
    out[:, pl.ds(pl.multiple_of((1 - core) * half, half), half)] = right.astype(BF)


pin = lax.optimization_barrier


def swap(a):
    return lax.ppermute(a, "core", [(0, 1), (1, 0)])


def body(
    key_rows,
    value_rows,
    query_rows,
    step_rates,
    fast_gate,
    fast_up,
    fast_down,
    out_gain,
    gate_input,
    out_weight,
):
    chips = lax.axis_size("x")
    place = jnp.stack([lax.axis_index(a).astype(jnp.int32) for a in ("core", "x")])
    tokens, width = key_rows.shape[1:]
    part = fast_gate.shape[1]
    rows = 3 * part
    mine = pl.pallas_call(
        pack_kernel,
        out_shape=jax.ShapeDtypeStruct((2 * tokens + part, width), BF),
        in_specs=[VMEM] * 4,
        out_specs=VMEM,
        compiler_params=PARAMS,
        name="pack",
    )(key_rows[0], value_rows[0], step_rates, fast_down[0])
    mine, out_weight = pin((mine, out_weight))
    theirs = swap(mine)
    count = lax.axis_size("hs")
    depth, half = out_weight.shape[0], out_weight.shape[1] // 2
    piece = lax.dynamic_slice_in_dim(out_weight, place[0] * half, half, 1)
    left = lax.all_to_all(
        jnp.broadcast_to(piece, (count, depth, half)), "hs", split_axis=0, concat_axis=0, tiled=True
    ).reshape(count * depth, half)
    weights = pl.pallas_call(
        choose_kernel,
        out_shape=jax.ShapeDtypeStruct((rows + 16, width), BF),
        in_specs=[SMEM] + [VMEM] * 4,
        out_specs=VMEM,
        compiler_params=PARAMS,
        name="choose",
    )(place, fast_gate[0], fast_up[0], fast_down[0], theirs)
    held = lax.all_gather(weights, "x", axis=0, tiled=False)
    sums = pl.pallas_call(
        grad_kernel,
        out_shape=(jax.ShapeDtypeStruct((rows, width), BF),) * chips,
        in_specs=[SMEM] + [VMEM] * 3,
        out_specs=(VMEM,) * chips,
        scratch_shapes=[
            pltpu.VMEM((width // 2, width), F32),
            pltpu.VMEM((width // 2, width), F32),
            pltpu.VMEM((width, width // 2), F32),
        ],
        compiler_params=PARAMS,
        name="grads",
    )(place, mine, theirs, held)
    parts = [
        lax.ppermute(a, "x", [(x, (x + r) % chips) for x in range(chips)]) if r else a
        for r, a in enumerate(sums)
    ]
    new = pl.pallas_call(
        rescale_kernel,
        out_shape=jax.ShapeDtypeStruct((rows, width), BF),
        in_specs=[VMEM] * 5,
        out_specs=VMEM,
        compiler_params=PARAMS,
        name="rescale",
    )(*parts, weights)
    own = lax.all_gather(new, "x", axis=0, tiled=False)
    own, left = pin((own, left))
    other = swap(own)
    right = swap(left)
    head_out = pl.pallas_call(
        query_kernel,
        out_shape=jax.ShapeDtypeStruct((tokens, width), BF),
        in_specs=[VMEM] * 4,
        out_specs=VMEM,
        compiler_params=PARAMS,
        name="query",
    )(query_rows[0], held, own, other)
    blocks = head_out.reshape(count, tokens // count, width)
    moved = lax.all_to_all(blocks, "hs", split_axis=0, concat_axis=0, tiled=True)
    few, seqs, model = gate_input.shape
    heads = model // width
    columns = out_weight.shape[1]
    result = pl.pallas_call(
        functools.partial(output_kernel, seqs=seqs, heads=heads),
        out_shape=jax.ShapeDtypeStruct((few * seqs, columns), BF),
        in_specs=[SMEM] + [VMEM] * 5,
        out_specs=VMEM,
        compiler_params=PARAMS,
        name="project",
    )(
        place,
        moved.reshape(tokens, width),
        out_gain.reshape(1, model),
        gate_input.reshape(few * seqs, model),
        left,
        right,
    )
    return result.reshape(few, seqs, columns)


def solution(mesh):
    ctx, pairs = mesh.devices.shape
    split = Mesh(mesh.devices.reshape(ctx // 2, 2, pairs), ("x", "core", "hs"))
    c = ("x", "core")
    return jax.shard_map(
        body,
        mesh=split,
        in_specs=(
            P("hs", c, None),
            P("hs", c, None),
            P("hs", c, None),
            P("hs", c),
            P("hs", c, None),
            P("hs", c, None),
            P("hs", c, None),
            P(),
            P(c + ("hs",), None, None),
            P("hs", None),
        ),
        out_specs=P(c + ("hs",), None, None),
        check_vma=False,
    )
```

```python
import functools

import jax
import jax.numpy as jnp
from jax import lax
from jax.experimental import pallas as pl
from jax.experimental.pallas import tpu as pltpu
from jax.sharding import Mesh
from jax.sharding import PartitionSpec as P

epsilon = 1e-06
BF = jnp.bfloat16
F32 = jnp.float32
VMEM = pl.BlockSpec(memory_space=pltpu.VMEM)
HBM = pl.BlockSpec(memory_space=pltpu.HBM)
SMEM = pl.BlockSpec(memory_space=pltpu.SMEM)
PARAMS = pltpu.CompilerParams(vmem_limit_bytes=20 * 1024 * 1024)


def dot(left, right, a, b):
    return lax.dot_general(left, right, (((a,), (b,)), ((), ())), preferred_element_type=F32)


def pack_kernel(key, value, rate, down, out, value_buf, rate_buf, sems):
    tokens, width = key.shape
    part = down.shape[0]
    copies = [
        pltpu.make_async_copy(rate, rate_buf, sems.at[0]),
        pltpu.make_async_copy(value, value_buf, sems.at[1]),
        pltpu.make_async_copy(key, out.at[pl.ds(0, tokens), :], sems.at[2]),
        pltpu.make_async_copy(down, out.at[pl.ds(2 * tokens, part), :], sems.at[3]),
    ]
    for copy in copies:
        copy.start()
    copies[0].wait()
    column = jnp.transpose(jnp.broadcast_to(rate_buf[...], (128, tokens)))
    copies[1].wait()
    out[tokens : 2 * tokens, :] = (
        jnp.concatenate([column] * (width // 128), axis=1) * value_buf[...].astype(F32)
    ).astype(BF)
    copies[2].wait()
    copies[3].wait()


def choose_kernel(place_ref, gate, up, down, other, out):
    core = place_ref[0]
    part, width = gate.shape
    half = width // 2
    out[:part, :] = gate[...]
    out[part : 2 * part, :] = up[...]
    own, theirs = down[...], other[...]
    first = core == 0
    rows = jnp.concatenate(
        [jnp.where(first, own.astype(F32), theirs.astype(F32)), jnp.where(first, theirs.astype(F32), own.astype(F32))],
        axis=0,
    )
    unit = lax.broadcasted_iota(jnp.int32, (width, half), 0)
    slot = lax.broadcasted_iota(jnp.int32, (width, half), 1)
    source = (slot // part * 2 + core) * part + slot % part
    chosen = dot(rows.astype(BF), jnp.where(unit == source, 1.0, 0.0).astype(BF), 1, 0).astype(BF)
    out[2 * part : 3 * part, :half] = chosen[:part, :]
    out[2 * part : 3 * part, half:] = chosen[part:, :]
    total = jnp.sum(rows * rows, -1, keepdims=True)
    total = jnp.transpose(jnp.broadcast_to(total, (2 * part, 128)))[:1, :]
    high = total.astype(BF).astype(F32)
    middle = (total - high).astype(BF).astype(F32)
    low = total - high - middle
    tail = out.shape[0] - 3 * part
    row = lax.broadcasted_iota(jnp.int32, (tail, 2 * part), 0)
    terms = jnp.where(row == 0, high, jnp.where(row == 1, middle, jnp.where(row == 2, low, 0.0)))
    out[3 * part :, :] = jnp.concatenate(
        [terms, jnp.zeros((tail, width - 2 * part), F32)], axis=1
    ).astype(BF)


def halves(held):
    chips, _, width = held.shape
    part = width // (2 * chips)
    half = width // 2
    gate = jnp.concatenate([held[x, :part, :] for x in range(chips)], axis=0)
    up = jnp.concatenate([held[x, part : 2 * part, :] for x in range(chips)], axis=0)
    down = jnp.concatenate(
        [
            held[x, 2 * part : 3 * part, c * half : (c + 1) * half]
            for x in range(chips)
            for c in range(2)
        ],
        axis=0,
    )
    return gate, up, down


def grad_kernel(place_ref, mine, theirs, held, o0, o1, o2, o3, g0, g1, g2, fetched, sem):
    gate, up, down = halves(held)
    chips, _, width = held.shape
    part = width // (2 * chips)
    half = width // 2
    tokens = width
    total = None
    copy = pltpu.make_async_copy(theirs.at[pl.ds(0, 2 * tokens), :], fetched, sem)
    copy.start()
    for rows in (mine, fetched):
        if rows is fetched:
            copy.wait()
        k, scaled = rows[:tokens, :], rows[tokens : 2 * tokens, :]
        pre_gate = dot(k, gate, 1, 1)
        pre_up = dot(k, up, 1, 1)
        back = dot(scaled, down, 1, 0)
        sig = jax.nn.sigmoid(pre_gate)
        act = pre_gate * sig
        hidden = (act * pre_up).astype(BF)
        back_gate = (back * pre_up * sig * (1.0 + pre_gate * (1.0 - sig))).astype(BF)
        back_up = (back * act).astype(BF)
        grads = (dot(back_gate, k, 0, 0), dot(back_up, k, 0, 0), dot(scaled, hidden, 0, 0))
        if total is None:
            g0[...], g1[...], g2[...] = grads
            total = grads
        else:
            for g, grad in zip((g0, g1, g2), grads):
                g[...] += grad
    for r, out in enumerate((o0, o1, o2, o3)):
        x = lax.rem(place_ref[1] + r, chips)
        spot = pl.multiple_of(x * part, part)
        out[:part, :] = g0[pl.ds(spot, part), :].astype(BF)
        out[part : 2 * part, :] = g1[pl.ds(spot, part), :].astype(BF)
        for c in range(2):
            spot = pl.multiple_of((2 * x + c) * part, part)
            out[2 * part :, c * half : (c + 1) * half] = g2[pl.ds(spot, part), :].astype(BF)


def rescale_kernel(p0, p1, p2, p3, weight, new):
    rows = p0.shape[0]
    whole = rows // 3 * 2
    base = weight[:rows, :].astype(F32)
    total = p0[...].astype(F32) + p1[...].astype(F32)
    moved = base + (total + (p2[...].astype(F32) + p3[...].astype(F32)))
    factor = jnp.sqrt(jnp.mean(base * base, -1, keepdims=True) + epsilon) / jnp.sqrt(
        jnp.mean(moved * moved, -1, keepdims=True) + epsilon
    )
    new[:whole, :] = (moved * factor)[:whole, :].astype(BF)
    new[whole:, :] = moved[whole:, :].astype(BF)


def query_kernel(query, held, own, other, out):
    chips, _, width = own.shape
    q = query[...]
    result = squares = None
    for rows in (own, other):
        gate, up, down = halves(rows)
        pre_gate = dot(q, gate, 1, 1)
        pre_up = dot(q, up, 1, 1)
        hidden = (pre_gate * jax.nn.sigmoid(pre_gate) * pre_up).astype(BF)
        part = dot(hidden, down, 1, 1)
        d = down.astype(F32)
        square = jnp.sum(d * d, -1, keepdims=True)
        result = part if result is None else result + part
        squares = square if squares is None else squares + square
    moved = jnp.transpose(jnp.broadcast_to(squares, (width, 128)))[:1, :]
    span = width // chips
    tail = own.shape[1]
    base = jnp.concatenate(
        [
            jnp.sum(held[x, tail:, :span].astype(F32), 0, keepdims=True)
            for x in range(chips)
        ],
        axis=1,
    )
    factor = jnp.sqrt(base * (1.0 / width) + epsilon) / jnp.sqrt(moved * (1.0 / width) + epsilon)
    out[...] = (result * factor).astype(BF)


def output_kernel(core_ref, moved, gain, gate, mine, theirs, out, *, seqs, heads):
    total, size = moved.shape
    rows = total // heads
    tokens = rows // seqs
    row = lax.broadcasted_iota(jnp.int32, (rows, total), 0)
    column = lax.broadcasted_iota(jnp.int32, (rows, total), 1)
    first = (row % seqs * heads) * tokens + row // seqs
    left = right = None
    for h in range(heads):
        pick = jnp.where(column == first + h * tokens, 1.0, 0.0).astype(BF)
        mixed = dot(pick, moved[...], 1, 0)
        square = jnp.mean(mixed * mixed, -1, keepdims=True)
        span = slice(h * size, (h + 1) * size)
        g = gate[:, span].astype(F32)
        normed = mixed * lax.rsqrt(square + epsilon) * gain[:, span] * (g * jax.nn.sigmoid(g))
        normed = normed.astype(BF)
        one, two = dot(normed, mine[span, :], 1, 0), dot(normed, theirs[span, :], 1, 0)
        left = one if left is None else left + one
        right = two if right is None else right + two
    half = mine.shape[1]
    core = core_ref[0]
    out[:, pl.ds(pl.multiple_of(core * half, half), half)] = left.astype(BF)
    out[:, pl.ds(pl.multiple_of((1 - core) * half, half), half)] = right.astype(BF)


pin = lax.optimization_barrier


def swap(a):
    return lax.ppermute(a, "core", [(0, 1), (1, 0)])


def body(
    key_rows,
    value_rows,
    query_rows,
    step_rates,
    fast_gate,
    fast_up,
    fast_down,
    out_gain,
    gate_input,
    out_weight,
):
    chips = lax.axis_size("x")
    place = jnp.stack([lax.axis_index(a).astype(jnp.int32) for a in ("core", "x")])
    tokens, width = key_rows.shape[1:]
    part = fast_gate.shape[1]
    rows = 3 * part
    mine = pl.pallas_call(
        pack_kernel,
        out_shape=jax.ShapeDtypeStruct((2 * tokens + part, width), BF),
        in_specs=[HBM] * 4,
        out_specs=VMEM,
        scratch_shapes=[
            pltpu.VMEM((tokens, width), BF),
            pltpu.VMEM((1, tokens), F32),
            pltpu.SemaphoreType.DMA((4,)),
        ],
        compiler_params=pltpu.CompilerParams(vmem_limit_bytes=60 * 1024 * 1024),
        name="pack",
    )(key_rows[0], value_rows[0], step_rates, fast_down[0])
    theirs = swap(mine)
    count = lax.axis_size("hs")
    depth, half = out_weight.shape[0], out_weight.shape[1] // 2
    piece = lax.dynamic_slice_in_dim(out_weight, place[0] * half, half, 1)
    pieces = jnp.broadcast_to(piece, (count, depth, half))
    pieces, theirs = pin((pieces, theirs))
    left = lax.all_to_all(pieces, "hs", split_axis=0, concat_axis=0, tiled=True).reshape(
        count * depth, half
    )
    weights = pl.pallas_call(
        choose_kernel,
        out_shape=jax.ShapeDtypeStruct((rows + 16, width), BF),
        in_specs=[SMEM] + [VMEM] * 4,
        out_specs=VMEM,
        compiler_params=PARAMS,
        name="choose",
    )(place, fast_gate[0], fast_up[0], fast_down[0], theirs[2 * tokens :])
    held = lax.all_gather(weights, "x", axis=0, tiled=False)
    sums = pl.pallas_call(
        grad_kernel,
        out_shape=(jax.ShapeDtypeStruct((rows, width), BF),) * chips,
        in_specs=[SMEM, VMEM, HBM, VMEM],
        out_specs=(VMEM,) * chips,
        scratch_shapes=[
            pltpu.VMEM((width // 2, width), F32),
            pltpu.VMEM((width // 2, width), F32),
            pltpu.VMEM((width, width // 2), F32),
            pltpu.VMEM((2 * tokens, width), BF),
            pltpu.SemaphoreType.DMA,
        ],
        compiler_params=PARAMS,
        name="grads",
    )(place, mine, theirs, held)
    parts = [
        lax.ppermute(a, "x", [(x, (x + r) % chips) for x in range(chips)]) if r else a
        for r, a in enumerate(sums)
    ]
    new = pl.pallas_call(
        rescale_kernel,
        out_shape=jax.ShapeDtypeStruct((rows, width), BF),
        in_specs=[VMEM] * 5,
        out_specs=VMEM,
        compiler_params=PARAMS,
        name="rescale",
    )(*parts, weights)
    own = lax.all_gather(new, "x", axis=0, tiled=False)
    other = swap(own)
    head_out = pl.pallas_call(
        query_kernel,
        out_shape=jax.ShapeDtypeStruct((tokens, width), BF),
        in_specs=[VMEM] * 4,
        out_specs=VMEM,
        compiler_params=PARAMS,
        name="query",
    )(query_rows[0], held, own, other)
    head_out, left = pin((head_out, left))
    right = swap(left)
    blocks = head_out.reshape(count, tokens // count, width)
    moved = lax.all_to_all(blocks, "hs", split_axis=0, concat_axis=0, tiled=True)
    few, seqs, model = gate_input.shape
    heads = model // width
    columns = out_weight.shape[1]
    result = pl.pallas_call(
        functools.partial(output_kernel, seqs=seqs, heads=heads),
        out_shape=jax.ShapeDtypeStruct((few * seqs, columns), BF),
        in_specs=[SMEM] + [VMEM] * 5,
        out_specs=VMEM,
        compiler_params=PARAMS,
        name="project",
    )(
        place,
        moved.reshape(tokens, width),
        out_gain.reshape(1, model),
        gate_input.reshape(few * seqs, model),
        left,
        right,
    )
    return result.reshape(few, seqs, columns)


def solution(mesh):
    ctx, pairs = mesh.devices.shape
    split = Mesh(mesh.devices.reshape(ctx // 2, 2, pairs), ("x", "core", "hs"))
    c = ("x", "core")
    return jax.shard_map(
        body,
        mesh=split,
        in_specs=(
            P("hs", c, None),
            P("hs", c, None),
            P("hs", c, None),
            P("hs", c),
            P("hs", c, None),
            P("hs", c, None),
            P("hs", c, None),
            P(),
            P(c + ("hs",), None, None),
            P("hs", None),
        ),
        out_specs=P(c + ("hs",), None, None),
        check_vma=False,
    )
```

```python
import functools

import jax
import jax.numpy as jnp
from jax import lax
from jax.experimental import pallas as pl
from jax.experimental.pallas import tpu as pltpu
from jax.sharding import Mesh
from jax.sharding import PartitionSpec as P

epsilon = 1e-06
BF = jnp.bfloat16
F32 = jnp.float32
VMEM = pl.BlockSpec(memory_space=pltpu.VMEM)
HBM = pl.BlockSpec(memory_space=pltpu.HBM)
SMEM = pl.BlockSpec(memory_space=pltpu.SMEM)
PARAMS = pltpu.CompilerParams(vmem_limit_bytes=20 * 1024 * 1024)


def dot(left, right, a, b):
    return lax.dot_general(left, right, (((a,), (b,)), ((), ())), preferred_element_type=F32)


def pack_kernel(key, value, rate, out, value_buf, rate_buf, sems):
    tokens, width = key.shape
    copies = [
        pltpu.make_async_copy(rate, rate_buf, sems.at[0]),
        pltpu.make_async_copy(value, value_buf, sems.at[1]),
        pltpu.make_async_copy(key, out.at[pl.ds(0, tokens), :], sems.at[2]),
    ]
    for copy in copies:
        copy.start()
    copies[0].wait()
    column = jnp.transpose(jnp.broadcast_to(rate_buf[...], (128, tokens)))
    copies[1].wait()
    out[tokens : 2 * tokens, :] = (
        jnp.concatenate([column] * (width // 128), axis=1) * value_buf[...].astype(F32)
    ).astype(BF)
    copies[2].wait()


def choose_kernel(place_ref, gate, up, down, other, out):
    core = place_ref[0]
    part, width = gate.shape
    half = width // 2
    out[:part, :] = gate[...]
    out[part : 2 * part, :] = up[...]
    own, theirs = down[...], other[...]
    first = core == 0
    rows = jnp.concatenate(
        [jnp.where(first, own.astype(F32), theirs.astype(F32)), jnp.where(first, theirs.astype(F32), own.astype(F32))],
        axis=0,
    )
    unit = lax.broadcasted_iota(jnp.int32, (width, half), 0)
    slot = lax.broadcasted_iota(jnp.int32, (width, half), 1)
    source = (slot // part * 2 + core) * part + slot % part
    chosen = dot(rows.astype(BF), jnp.where(unit == source, 1.0, 0.0).astype(BF), 1, 0).astype(BF)
    out[2 * part : 3 * part, :half] = chosen[:part, :]
    out[2 * part : 3 * part, half:] = chosen[part:, :]
    total = jnp.sum(rows * rows, -1, keepdims=True)
    total = jnp.transpose(jnp.broadcast_to(total, (2 * part, 128)))[:1, :]
    high = total.astype(BF).astype(F32)
    middle = (total - high).astype(BF).astype(F32)
    low = total - high - middle
    tail = out.shape[0] - 3 * part
    row = lax.broadcasted_iota(jnp.int32, (tail, 2 * part), 0)
    terms = jnp.where(row == 0, high, jnp.where(row == 1, middle, jnp.where(row == 2, low, 0.0)))
    out[3 * part :, :] = jnp.concatenate(
        [terms, jnp.zeros((tail, width - 2 * part), F32)], axis=1
    ).astype(BF)


def halves(held):
    chips, _, width = held.shape
    part = width // (2 * chips)
    half = width // 2
    gate = jnp.concatenate([held[x, :part, :] for x in range(chips)], axis=0)
    up = jnp.concatenate([held[x, part : 2 * part, :] for x in range(chips)], axis=0)
    down = jnp.concatenate(
        [
            held[x, 2 * part : 3 * part, c * half : (c + 1) * half]
            for x in range(chips)
            for c in range(2)
        ],
        axis=0,
    )
    return gate, up, down


def grad_kernel(place_ref, mine, theirs, held, o0, o1, o2, o3, g0, g1, g2, fetched, sem):
    gate, up, down = halves(held)
    chips, _, width = held.shape
    part = width // (2 * chips)
    half = width // 2
    tokens = width
    found = []
    copy = pltpu.make_async_copy(theirs, fetched, sem)
    copy.start()
    for rows in (mine, fetched):
        if rows is fetched:
            copy.wait()
        k, scaled = rows[:tokens, :], rows[tokens:, :]
        pre_gate = dot(k, gate, 1, 1)
        pre_up = dot(k, up, 1, 1)
        back = dot(scaled, down, 1, 0)
        sig = jax.nn.sigmoid(pre_gate)
        act = pre_gate * sig
        hidden = (act * pre_up).astype(BF)
        back_gate = (back * pre_up * sig * (1.0 + pre_gate * (1.0 - sig))).astype(BF)
        back_up = (back * act).astype(BF)
        found.append((dot(back_gate, k, 0, 0), dot(back_up, k, 0, 0), dot(scaled, hidden, 0, 0)))
    for g, one, two in zip((g0, g1, g2), *found):
        g[...] = (one + two).astype(BF)
    for r, out in enumerate((o0, o1, o2, o3)):
        x = lax.rem(place_ref[1] + r, chips)
        spot = pl.multiple_of(x * part, part)
        out[:part, :] = g0[pl.ds(spot, part), :]
        out[part : 2 * part, :] = g1[pl.ds(spot, part), :]
        for c in range(2):
            spot = pl.multiple_of((2 * x + c) * part, part)
            out[2 * part :, c * half : (c + 1) * half] = g2[pl.ds(spot, part), :]


def rescale_kernel(p0, p1, p2, p3, weight, new):
    rows = p0.shape[0]
    whole = rows // 3 * 2
    base = weight[:rows, :].astype(F32)
    total = p0[...].astype(F32) + p1[...].astype(F32)
    moved = base + (total + (p2[...].astype(F32) + p3[...].astype(F32)))
    factor = jnp.sqrt(jnp.mean(base * base, -1, keepdims=True) + epsilon) / jnp.sqrt(
        jnp.mean(moved * moved, -1, keepdims=True) + epsilon
    )
    new[:whole, :] = (moved * factor)[:whole, :].astype(BF)
    new[whole:, :] = moved[whole:, :].astype(BF)


def query_kernel(query, held, own, other, out):
    chips, _, width = own.shape
    q = query[...]
    result = squares = None
    for rows in (own, other):
        gate, up, down = halves(rows)
        pre_gate = dot(q, gate, 1, 1)
        pre_up = dot(q, up, 1, 1)
        hidden = (pre_gate * jax.nn.sigmoid(pre_gate) * pre_up).astype(BF)
        part = dot(hidden, down, 1, 1)
        d = down.astype(F32)
        square = jnp.sum(d * d, -1, keepdims=True)
        result = part if result is None else result + part
        squares = square if squares is None else squares + square
    moved = jnp.transpose(jnp.broadcast_to(squares, (width, 128)))[:1, :]
    span = width // chips
    tail = own.shape[1]
    base = jnp.concatenate(
        [
            jnp.sum(held[x, tail:, :span].astype(F32), 0, keepdims=True)
            for x in range(chips)
        ],
        axis=1,
    )
    factor = jnp.sqrt(base * (1.0 / width) + epsilon) / jnp.sqrt(moved * (1.0 / width) + epsilon)
    out[...] = (result * factor).astype(BF)


def output_kernel(core_ref, moved, gain, gate, mine, theirs, out, *, seqs, heads):
    total, size = moved.shape
    rows = total // heads
    tokens = rows // seqs
    row = lax.broadcasted_iota(jnp.int32, (rows, total), 0)
    column = lax.broadcasted_iota(jnp.int32, (rows, total), 1)
    first = (row % seqs * heads) * tokens + row // seqs
    left = right = None
    for h in range(heads):
        pick = jnp.where(column == first + h * tokens, 1.0, 0.0).astype(BF)
        mixed = dot(pick, moved[...], 1, 0)
        square = jnp.mean(mixed * mixed, -1, keepdims=True)
        span = slice(h * size, (h + 1) * size)
        g = gate[:, span].astype(F32)
        normed = mixed * lax.rsqrt(square + epsilon) * gain[:, span] * (g * jax.nn.sigmoid(g))
        normed = normed.astype(BF)
        one, two = dot(normed, mine[span, :], 1, 0), dot(normed, theirs[span, :], 1, 0)
        left = one if left is None else left + one
        right = two if right is None else right + two
    half = mine.shape[1]
    core = core_ref[0]
    out[:, pl.ds(pl.multiple_of(core * half, half), half)] = left.astype(BF)
    out[:, pl.ds(pl.multiple_of((1 - core) * half, half), half)] = right.astype(BF)


pin = lax.optimization_barrier


def swap(a):
    return lax.ppermute(a, "core", [(0, 1), (1, 0)])


def body(
    key_rows,
    value_rows,
    query_rows,
    step_rates,
    fast_gate,
    fast_up,
    fast_down,
    out_gain,
    gate_input,
    out_weight,
):
    chips = lax.axis_size("x")
    place = jnp.stack([lax.axis_index(a).astype(jnp.int32) for a in ("core", "x")])
    tokens, width = key_rows.shape[1:]
    part = fast_gate.shape[1]
    rows = 3 * part
    mine = pl.pallas_call(
        pack_kernel,
        out_shape=jax.ShapeDtypeStruct((2 * tokens, width), BF),
        in_specs=[HBM] * 3,
        out_specs=VMEM,
        scratch_shapes=[
            pltpu.VMEM((tokens, width), BF),
            pltpu.VMEM((1, tokens), F32),
            pltpu.SemaphoreType.DMA((3,)),
        ],
        compiler_params=pltpu.CompilerParams(vmem_limit_bytes=60 * 1024 * 1024),
        name="pack",
    )(key_rows[0], value_rows[0], step_rates)
    mine, other_down = pin((mine, swap(fast_down[0])))
    theirs = swap(mine)
    count = lax.axis_size("hs")
    depth, half = out_weight.shape[0], out_weight.shape[1] // 2
    piece = lax.dynamic_slice_in_dim(out_weight, place[0] * half, half, 1)
    pieces = jnp.broadcast_to(piece, (count, depth, half))
    left = lax.all_to_all(pieces, "hs", split_axis=0, concat_axis=0, tiled=True).reshape(
        count * depth, half
    )
    weights = pl.pallas_call(
        choose_kernel,
        out_shape=jax.ShapeDtypeStruct((rows + 16, width), BF),
        in_specs=[SMEM] + [VMEM] * 4,
        out_specs=VMEM,
        compiler_params=PARAMS,
        name="choose",
    )(place, fast_gate[0], fast_up[0], fast_down[0], other_down)
    held = lax.all_gather(weights, "x", axis=0, tiled=False)
    sums = pl.pallas_call(
        grad_kernel,
        out_shape=(jax.ShapeDtypeStruct((rows, width), BF),) * chips,
        in_specs=[SMEM, VMEM, HBM, VMEM],
        out_specs=(VMEM,) * chips,
        scratch_shapes=[
            pltpu.VMEM((width // 2, width), BF),
            pltpu.VMEM((width // 2, width), BF),
            pltpu.VMEM((width, width // 2), BF),
            pltpu.VMEM((2 * tokens, width), BF),
            pltpu.SemaphoreType.DMA,
        ],
        compiler_params=PARAMS,
        name="grads",
    )(place, mine, theirs, held)
    parts = [
        lax.ppermute(a, "x", [(x, (x + r) % chips) for x in range(chips)]) if r else a
        for r, a in enumerate(sums)
    ]
    new = pl.pallas_call(
        rescale_kernel,
        out_shape=jax.ShapeDtypeStruct((rows, width), BF),
        in_specs=[VMEM] * 5,
        out_specs=VMEM,
        compiler_params=PARAMS,
        name="rescale",
    )(*parts, weights)
    own = lax.all_gather(new, "x", axis=0, tiled=False)
    other = swap(own)
    head_out = pl.pallas_call(
        query_kernel,
        out_shape=jax.ShapeDtypeStruct((tokens, width), BF),
        in_specs=[VMEM] * 4,
        out_specs=VMEM,
        compiler_params=PARAMS,
        name="query",
    )(query_rows[0], held, own, other)
    head_out, left = pin((head_out, left))
    right = swap(left)
    blocks = head_out.reshape(count, tokens // count, width)
    moved = lax.all_to_all(blocks, "hs", split_axis=0, concat_axis=0, tiled=True)
    few, seqs, model = gate_input.shape
    heads = model // width
    columns = out_weight.shape[1]
    result = pl.pallas_call(
        functools.partial(output_kernel, seqs=seqs, heads=heads),
        out_shape=jax.ShapeDtypeStruct((few * seqs, columns), BF),
        in_specs=[SMEM] + [VMEM] * 5,
        out_specs=VMEM,
        compiler_params=PARAMS,
        name="project",
    )(
        place,
        moved.reshape(tokens, width),
        out_gain.reshape(1, model),
        gate_input.reshape(few * seqs, model),
        left,
        right,
    )
    return result.reshape(few, seqs, columns)


def solution(mesh):
    ctx, pairs = mesh.devices.shape
    split = Mesh(mesh.devices.reshape(ctx // 2, 2, pairs), ("x", "core", "hs"))
    c = ("x", "core")
    return jax.shard_map(
        body,
        mesh=split,
        in_specs=(
            P("hs", c, None),
            P("hs", c, None),
            P("hs", c, None),
            P("hs", c),
            P("hs", c, None),
            P("hs", c, None),
            P("hs", c, None),
            P(),
            P(c + ("hs",), None, None),
            P("hs", None),
        ),
        out_specs=P(c + ("hs",), None, None),
        check_vma=False,
    )
```

```python
import functools

import jax
import jax.numpy as jnp
from jax import lax
from jax.experimental import pallas as pl
from jax.experimental.pallas import tpu as pltpu
from jax.sharding import Mesh
from jax.sharding import PartitionSpec as P

epsilon = 1e-06
BF = jnp.bfloat16
F32 = jnp.float32
VMEM = pl.BlockSpec(memory_space=pltpu.VMEM)
HBM = pl.BlockSpec(memory_space=pltpu.HBM)
SMEM = pl.BlockSpec(memory_space=pltpu.SMEM)
PARAMS = pltpu.CompilerParams(vmem_limit_bytes=20 * 1024 * 1024)


def dot(left, right, a, b):
    return lax.dot_general(left, right, (((a,), (b,)), ((), ())), preferred_element_type=F32)


def pack_kernel(key, value, rate, out, value_buf, rate_buf, sems):
    tokens, width = key.shape
    copies = [
        pltpu.make_async_copy(rate, rate_buf, sems.at[0]),
        pltpu.make_async_copy(value, value_buf, sems.at[1]),
        pltpu.make_async_copy(key, out.at[pl.ds(0, tokens), :], sems.at[2]),
    ]
    for copy in copies:
        copy.start()
    copies[0].wait()
    column = jnp.transpose(jnp.broadcast_to(rate_buf[...], (128, tokens)))
    copies[1].wait()
    out[tokens : 2 * tokens, :] = (
        jnp.concatenate([column] * (width // 128), axis=1) * value_buf[...].astype(F32)
    ).astype(BF)
    copies[2].wait()


def choose_kernel(place_ref, gate, up, down, other, out):
    core = place_ref[0]
    part, width = gate.shape
    half = width // 2
    out[:part, :] = gate[...]
    out[part : 2 * part, :] = up[...]
    own, theirs = down[...], other[...]
    first = core == 0
    rows = jnp.concatenate(
        [jnp.where(first, own.astype(F32), theirs.astype(F32)), jnp.where(first, theirs.astype(F32), own.astype(F32))],
        axis=0,
    )
    unit = lax.broadcasted_iota(jnp.int32, (width, half), 0)
    slot = lax.broadcasted_iota(jnp.int32, (width, half), 1)
    source = (slot // part * 2 + core) * part + slot % part
    chosen = dot(rows.astype(BF), jnp.where(unit == source, 1.0, 0.0).astype(BF), 1, 0).astype(BF)
    out[2 * part : 3 * part, :half] = chosen[:part, :]
    out[2 * part : 3 * part, half:] = chosen[part:, :]
    total = jnp.sum(rows * rows, -1, keepdims=True)
    total = jnp.transpose(jnp.broadcast_to(total, (2 * part, 128)))[:1, :]
    high = total.astype(BF).astype(F32)
    middle = (total - high).astype(BF).astype(F32)
    low = total - high - middle
    tail = out.shape[0] - 3 * part
    row = lax.broadcasted_iota(jnp.int32, (tail, 2 * part), 0)
    terms = jnp.where(row == 0, high, jnp.where(row == 1, middle, jnp.where(row == 2, low, 0.0)))
    out[3 * part :, :] = jnp.concatenate(
        [terms, jnp.zeros((tail, width - 2 * part), F32)], axis=1
    ).astype(BF)


def halves(held):
    chips, _, width = held.shape
    part = width // (2 * chips)
    half = width // 2
    gate = jnp.concatenate([held[x, :part, :] for x in range(chips)], axis=0)
    up = jnp.concatenate([held[x, part : 2 * part, :] for x in range(chips)], axis=0)
    down = jnp.concatenate(
        [
            held[x, 2 * part : 3 * part, c * half : (c + 1) * half]
            for x in range(chips)
            for c in range(2)
        ],
        axis=0,
    )
    return gate, up, down


def grad_kernel(
    place_ref, mine, theirs, held, o0, o1, o2, o3, g0, g1, g2, keys, values, bg, bu, hid, sems
):
    chips, _, width = held.shape
    part = width // (2 * chips)
    half = width // 2
    tokens = width
    copies = [
        pltpu.make_async_copy(
            source.at[pl.ds(j * tokens, tokens), :],
            target.at[pl.ds(i * tokens, tokens), :],
            sems.at[i, j],
        )
        for i, source in enumerate((mine, theirs))
        for j, target in enumerate((keys, values))
    ]
    for copy in copies:
        copy.start()
    gate, up, down = halves(held)
    for i in range(2):
        if i:
            for copy in copies:
                copy.wait()
            k, scaled = keys[tokens:, :], values[tokens:, :]
        else:
            k, scaled = mine[:tokens, :], mine[tokens:, :]
        pre_gate = dot(k, gate, 1, 1)
        pre_up = dot(k, up, 1, 1)
        back = dot(scaled, down, 1, 0)
        sig = jax.nn.sigmoid(pre_gate)
        act = pre_gate * sig
        span = slice(i * tokens, (i + 1) * tokens)
        hid[span, :] = (act * pre_up).astype(BF)
        bg[span, :] = (back * pre_up * sig * (1.0 + pre_gate * (1.0 - sig))).astype(BF)
        bu[span, :] = (back * act).astype(BF)
    g0[...] = dot(bg[...], keys[...], 0, 0).astype(BF)
    g1[...] = dot(bu[...], keys[...], 0, 0).astype(BF)
    g2[...] = dot(values[...], hid[...], 0, 0).astype(BF)
    for r, out in enumerate((o0, o1, o2, o3)):
        x = lax.rem(place_ref[1] + r, chips)
        spot = pl.multiple_of(x * part, part)
        out[:part, :] = g0[pl.ds(spot, part), :]
        out[part : 2 * part, :] = g1[pl.ds(spot, part), :]
        for c in range(2):
            spot = pl.multiple_of((2 * x + c) * part, part)
            out[2 * part :, c * half : (c + 1) * half] = g2[pl.ds(spot, part), :]


def rescale_kernel(p0, p1, p2, p3, weight, new):
    rows = p0.shape[0]
    whole = rows // 3 * 2
    base = weight[:rows, :].astype(F32)
    total = p0[...].astype(F32) + p1[...].astype(F32)
    moved = base + (total + (p2[...].astype(F32) + p3[...].astype(F32)))
    factor = jnp.sqrt(jnp.mean(base * base, -1, keepdims=True) + epsilon) / jnp.sqrt(
        jnp.mean(moved * moved, -1, keepdims=True) + epsilon
    )
    new[:whole, :] = (moved * factor)[:whole, :].astype(BF)
    new[whole:, :] = moved[whole:, :].astype(BF)


def query_kernel(query, held, own, other, out):
    chips, _, width = own.shape
    q = query[...]
    result = squares = None
    for rows in (own, other):
        gate, up, down = halves(rows)
        pre_gate = dot(q, gate, 1, 1)
        pre_up = dot(q, up, 1, 1)
        hidden = (pre_gate * jax.nn.sigmoid(pre_gate) * pre_up).astype(BF)
        part = dot(hidden, down, 1, 1)
        d = down.astype(F32)
        square = jnp.sum(d * d, -1, keepdims=True)
        result = part if result is None else result + part
        squares = square if squares is None else squares + square
    moved = jnp.transpose(jnp.broadcast_to(squares, (width, 128)))[:1, :]
    span = width // chips
    tail = own.shape[1]
    base = jnp.concatenate(
        [
            jnp.sum(held[x, tail:, :span].astype(F32), 0, keepdims=True)
            for x in range(chips)
        ],
        axis=1,
    )
    factor = jnp.sqrt(base * (1.0 / width) + epsilon) / jnp.sqrt(moved * (1.0 / width) + epsilon)
    out[...] = (result * factor).astype(BF)


def output_kernel(core_ref, moved, gain, gate, mine, theirs, out, *, seqs, heads):
    total, size = moved.shape
    rows = total // heads
    tokens = rows // seqs
    row = lax.broadcasted_iota(jnp.int32, (rows, total), 0)
    column = lax.broadcasted_iota(jnp.int32, (rows, total), 1)
    first = (row % seqs * heads) * tokens + row // seqs
    left = right = None
    for h in range(heads):
        pick = jnp.where(column == first + h * tokens, 1.0, 0.0).astype(BF)
        mixed = dot(pick, moved[...], 1, 0)
        square = jnp.mean(mixed * mixed, -1, keepdims=True)
        span = slice(h * size, (h + 1) * size)
        g = gate[:, span].astype(F32)
        normed = mixed * lax.rsqrt(square + epsilon) * gain[:, span] * (g * jax.nn.sigmoid(g))
        normed = normed.astype(BF)
        one, two = dot(normed, mine[span, :], 1, 0), dot(normed, theirs[span, :], 1, 0)
        left = one if left is None else left + one
        right = two if right is None else right + two
    half = mine.shape[1]
    core = core_ref[0]
    out[:, pl.ds(pl.multiple_of(core * half, half), half)] = left.astype(BF)
    out[:, pl.ds(pl.multiple_of((1 - core) * half, half), half)] = right.astype(BF)


pin = lax.optimization_barrier


def swap(a):
    return lax.ppermute(a, "core", [(0, 1), (1, 0)])


def body(
    key_rows,
    value_rows,
    query_rows,
    step_rates,
    fast_gate,
    fast_up,
    fast_down,
    out_gain,
    gate_input,
    out_weight,
):
    chips = lax.axis_size("x")
    place = jnp.stack([lax.axis_index(a).astype(jnp.int32) for a in ("core", "x")])
    tokens, width = key_rows.shape[1:]
    part = fast_gate.shape[1]
    rows = 3 * part
    mine = pl.pallas_call(
        pack_kernel,
        out_shape=jax.ShapeDtypeStruct((2 * tokens, width), BF),
        in_specs=[HBM] * 3,
        out_specs=VMEM,
        scratch_shapes=[
            pltpu.VMEM((tokens, width), BF),
            pltpu.VMEM((1, tokens), F32),
            pltpu.SemaphoreType.DMA((3,)),
        ],
        compiler_params=pltpu.CompilerParams(vmem_limit_bytes=60 * 1024 * 1024),
        name="pack",
    )(key_rows[0], value_rows[0], step_rates)
    mine, other_down = pin((mine, swap(fast_down[0])))
    theirs = swap(mine)
    count = lax.axis_size("hs")
    depth, half = out_weight.shape[0], out_weight.shape[1] // 2
    piece = lax.dynamic_slice_in_dim(out_weight, place[0] * half, half, 1)
    pieces = jnp.broadcast_to(piece, (count, depth, half))
    left = lax.all_to_all(pieces, "hs", split_axis=0, concat_axis=0, tiled=True).reshape(
        count * depth, half
    )
    weights = pl.pallas_call(
        choose_kernel,
        out_shape=jax.ShapeDtypeStruct((rows + 16, width), BF),
        in_specs=[SMEM] + [VMEM] * 4,
        out_specs=VMEM,
        compiler_params=PARAMS,
        name="choose",
    )(place, fast_gate[0], fast_up[0], fast_down[0], other_down)
    held = lax.all_gather(weights, "x", axis=0, tiled=False)
    sums = pl.pallas_call(
        grad_kernel,
        out_shape=(jax.ShapeDtypeStruct((rows, width), BF),) * chips,
        in_specs=[SMEM, VMEM, HBM, VMEM],
        out_specs=(VMEM,) * chips,
        scratch_shapes=[
            pltpu.VMEM((width // 2, width), BF),
            pltpu.VMEM((width // 2, width), BF),
            pltpu.VMEM((width, width // 2), BF),
            pltpu.VMEM((2 * tokens, width), BF),
            pltpu.VMEM((2 * tokens, width), BF),
            pltpu.VMEM((2 * tokens, width // 2), BF),
            pltpu.VMEM((2 * tokens, width // 2), BF),
            pltpu.VMEM((2 * tokens, width // 2), BF),
            pltpu.SemaphoreType.DMA((2, 2)),
        ],
        compiler_params=PARAMS,
        name="grads",
    )(place, mine, theirs, held)
    parts = [
        lax.ppermute(a, "x", [(x, (x + r) % chips) for x in range(chips)]) if r else a
        for r, a in enumerate(sums)
    ]
    new = pl.pallas_call(
        rescale_kernel,
        out_shape=jax.ShapeDtypeStruct((rows, width), BF),
        in_specs=[VMEM] * 5,
        out_specs=VMEM,
        compiler_params=PARAMS,
        name="rescale",
    )(*parts, weights)
    own = lax.all_gather(new, "x", axis=0, tiled=False)
    other = swap(own)
    head_out = pl.pallas_call(
        query_kernel,
        out_shape=jax.ShapeDtypeStruct((tokens, width), BF),
        in_specs=[VMEM] * 4,
        out_specs=VMEM,
        compiler_params=PARAMS,
        name="query",
    )(query_rows[0], held, own, other)
    head_out, left = pin((head_out, left))
    right = swap(left)
    blocks = head_out.reshape(count, tokens // count, width)
    moved = lax.all_to_all(blocks, "hs", split_axis=0, concat_axis=0, tiled=True)
    few, seqs, model = gate_input.shape
    heads = model // width
    columns = out_weight.shape[1]
    result = pl.pallas_call(
        functools.partial(output_kernel, seqs=seqs, heads=heads),
        out_shape=jax.ShapeDtypeStruct((few * seqs, columns), BF),
        in_specs=[SMEM] + [VMEM] * 5,
        out_specs=VMEM,
        compiler_params=PARAMS,
        name="project",
    )(
        place,
        moved.reshape(tokens, width),
        out_gain.reshape(1, model),
        gate_input.reshape(few * seqs, model),
        left,
        right,
    )
    return result.reshape(few, seqs, columns)


def solution(mesh):
    ctx, pairs = mesh.devices.shape
    split = Mesh(mesh.devices.reshape(ctx // 2, 2, pairs), ("x", "core", "hs"))
    c = ("x", "core")
    return jax.shard_map(
        body,
        mesh=split,
        in_specs=(
            P("hs", c, None),
            P("hs", c, None),
            P("hs", c, None),
            P("hs", c),
            P("hs", c, None),
            P("hs", c, None),
            P("hs", c, None),
            P(),
            P(c + ("hs",), None, None),
            P("hs", None),
        ),
        out_specs=P(c + ("hs",), None, None),
        check_vma=False,
    )
```

```python
import functools

import jax
import jax.numpy as jnp
from jax import lax
from jax.experimental import pallas as pl
from jax.experimental.pallas import tpu as pltpu
from jax.sharding import Mesh
from jax.sharding import PartitionSpec as P

epsilon = 1e-06
BF = jnp.bfloat16
F32 = jnp.float32
VMEM = pl.BlockSpec(memory_space=pltpu.VMEM)
HBM = pl.BlockSpec(memory_space=pltpu.HBM)
SMEM = pl.BlockSpec(memory_space=pltpu.SMEM)
PARAMS = pltpu.CompilerParams(vmem_limit_bytes=20 * 1024 * 1024)


def dot(left, right, a, b):
    return lax.dot_general(left, right, (((a,), (b,)), ((), ())), preferred_element_type=F32)


def pack_kernel(
    place_ref, key, value, rate, down, weight, out, pieces, value_buf, rate_buf, repeated, sems, more
):
    tokens, width = key.shape
    part = down.shape[0]
    copies = [
        pltpu.make_async_copy(rate, rate_buf, sems.at[0]),
        pltpu.make_async_copy(value, value_buf, sems.at[1]),
        pltpu.make_async_copy(key, out.at[pl.ds(0, tokens), :], sems.at[2]),
        pltpu.make_async_copy(down, out.at[pl.ds(2 * tokens, part), :], sems.at[3]),
    ]
    few, _, half = repeated.shape
    start = pl.multiple_of(place_ref[0] * half, half)
    fetch = pltpu.make_async_copy(weight.at[:, pl.ds(start, half)], repeated.at[0], sems.at[4])
    fetch.start()
    for copy in copies:
        copy.start()
    fetch.wait()
    for i in range(1, few):
        repeated[i] = repeated[0]
    outs = [
        pltpu.make_async_copy(repeated, pieces.at[pl.ds(i * few, few)], more.at[i])
        for i in range(pieces.shape[0] // few)
    ]
    for copy in outs:
        copy.start()
    copies[0].wait()
    column = jnp.transpose(jnp.broadcast_to(rate_buf[...], (128, tokens)))
    copies[1].wait()
    out[tokens : 2 * tokens, :] = (
        jnp.concatenate([column] * (width // 128), axis=1) * value_buf[...].astype(F32)
    ).astype(BF)
    copies[2].wait()
    copies[3].wait()
    for copy in outs:
        copy.wait()


def tail_kernel(rows, out):
    out[...] = rows[rows.shape[0] - out.shape[0] :, :]


def choose_kernel(place_ref, gate, up, down, other, out):
    core = place_ref[0]
    part, width = gate.shape
    half = width // 2
    out[:part, :] = gate[...]
    out[part : 2 * part, :] = up[...]
    own, theirs = down[...], other[...]
    first = core == 0
    rows = jnp.concatenate(
        [jnp.where(first, own.astype(F32), theirs.astype(F32)), jnp.where(first, theirs.astype(F32), own.astype(F32))],
        axis=0,
    )
    unit = lax.broadcasted_iota(jnp.int32, (width, half), 0)
    slot = lax.broadcasted_iota(jnp.int32, (width, half), 1)
    source = (slot // part * 2 + core) * part + slot % part
    chosen = dot(rows.astype(BF), jnp.where(unit == source, 1.0, 0.0).astype(BF), 1, 0).astype(BF)
    out[2 * part : 3 * part, :half] = chosen[:part, :]
    out[2 * part : 3 * part, half:] = chosen[part:, :]
    total = jnp.sum(rows * rows, -1, keepdims=True)
    total = jnp.transpose(jnp.broadcast_to(total, (2 * part, 128)))[:1, :]
    high = total.astype(BF).astype(F32)
    middle = (total - high).astype(BF).astype(F32)
    low = total - high - middle
    tail = out.shape[0] - 3 * part
    row = lax.broadcasted_iota(jnp.int32, (tail, 2 * part), 0)
    terms = jnp.where(row == 0, high, jnp.where(row == 1, middle, jnp.where(row == 2, low, 0.0)))
    out[3 * part :, :] = jnp.concatenate(
        [terms, jnp.zeros((tail, width - 2 * part), F32)], axis=1
    ).astype(BF)


def halves(held):
    chips, _, width = held.shape
    part = width // (2 * chips)
    half = width // 2
    gate = jnp.concatenate([held[x, :part, :] for x in range(chips)], axis=0)
    up = jnp.concatenate([held[x, part : 2 * part, :] for x in range(chips)], axis=0)
    down = jnp.concatenate(
        [
            held[x, 2 * part : 3 * part, c * half : (c + 1) * half]
            for x in range(chips)
            for c in range(2)
        ],
        axis=0,
    )
    return gate, up, down


def grad_kernel(
    place_ref, mine, theirs, held, o0, o1, o2, o3, g0, g1, g2, keys, values, bg, bu, hid, sems
):
    chips, _, width = held.shape
    part = width // (2 * chips)
    half = width // 2
    tokens = width
    copies = [
        pltpu.make_async_copy(
            source.at[pl.ds(j * tokens, tokens), :],
            target.at[pl.ds(i * tokens, tokens), :],
            sems.at[i, j],
        )
        for i, source in enumerate((mine, theirs))
        for j, target in enumerate((keys, values))
    ]
    for copy in copies:
        copy.start()
    gate, up, down = halves(held)
    for i in range(2):
        if i:
            for copy in copies:
                copy.wait()
            k, scaled = keys[tokens:, :], values[tokens:, :]
        else:
            k, scaled = mine[:tokens, :], mine[tokens : 2 * tokens, :]
        pre_gate = dot(k, gate, 1, 1)
        pre_up = dot(k, up, 1, 1)
        back = dot(scaled, down, 1, 0)
        sig = jax.nn.sigmoid(pre_gate)
        act = pre_gate * sig
        span = slice(i * tokens, (i + 1) * tokens)
        hid[span, :] = (act * pre_up).astype(BF)
        bg[span, :] = (back * pre_up * sig * (1.0 + pre_gate * (1.0 - sig))).astype(BF)
        bu[span, :] = (back * act).astype(BF)
    g0[...] = dot(bg[...], keys[...], 0, 0).astype(BF)
    g1[...] = dot(bu[...], keys[...], 0, 0).astype(BF)
    g2[...] = dot(values[...], hid[...], 0, 0).astype(BF)
    for r, out in enumerate((o0, o1, o2, o3)):
        x = lax.rem(place_ref[1] + r, chips)
        spot = pl.multiple_of(x * part, part)
        out[:part, :] = g0[pl.ds(spot, part), :]
        out[part : 2 * part, :] = g1[pl.ds(spot, part), :]
        for c in range(2):
            spot = pl.multiple_of((2 * x + c) * part, part)
            out[2 * part :, c * half : (c + 1) * half] = g2[pl.ds(spot, part), :]


def rescale_kernel(p0, p1, p2, p3, weight, new):
    rows = p0.shape[0]
    whole = rows // 3 * 2
    base = weight[:rows, :].astype(F32)
    total = p0[...].astype(F32) + p1[...].astype(F32)
    moved = base + (total + (p2[...].astype(F32) + p3[...].astype(F32)))
    factor = jnp.sqrt(jnp.mean(base * base, -1, keepdims=True) + epsilon) / jnp.sqrt(
        jnp.mean(moved * moved, -1, keepdims=True) + epsilon
    )
    new[:whole, :] = (moved * factor)[:whole, :].astype(BF)
    new[whole:, :] = moved[whole:, :].astype(BF)


def query_kernel(query, held, own, other, out):
    chips, _, width = own.shape
    q = query[...]
    result = squares = None
    for rows in (own, other):
        gate, up, down = halves(rows)
        pre_gate = dot(q, gate, 1, 1)
        pre_up = dot(q, up, 1, 1)
        hidden = (pre_gate * jax.nn.sigmoid(pre_gate) * pre_up).astype(BF)
        part = dot(hidden, down, 1, 1)
        d = down.astype(F32)
        square = jnp.sum(d * d, -1, keepdims=True)
        result = part if result is None else result + part
        squares = square if squares is None else squares + square
    moved = jnp.transpose(jnp.broadcast_to(squares, (width, 128)))[:1, :]
    span = width // chips
    tail = own.shape[1]
    base = jnp.concatenate(
        [
            jnp.sum(held[x, tail:, :span].astype(F32), 0, keepdims=True)
            for x in range(chips)
        ],
        axis=1,
    )
    factor = jnp.sqrt(base * (1.0 / width) + epsilon) / jnp.sqrt(moved * (1.0 / width) + epsilon)
    out[...] = (result * factor).astype(BF)


def output_kernel(core_ref, moved, gain, gate, mine, theirs, out, *, seqs, heads):
    total, size = moved.shape
    rows = total // heads
    tokens = rows // seqs
    row = lax.broadcasted_iota(jnp.int32, (rows, total), 0)
    column = lax.broadcasted_iota(jnp.int32, (rows, total), 1)
    first = (row % seqs * heads) * tokens + row // seqs
    left = right = None
    for h in range(heads):
        pick = jnp.where(column == first + h * tokens, 1.0, 0.0).astype(BF)
        mixed = dot(pick, moved[...], 1, 0)
        square = jnp.mean(mixed * mixed, -1, keepdims=True)
        span = slice(h * size, (h + 1) * size)
        g = gate[:, span].astype(F32)
        normed = mixed * lax.rsqrt(square + epsilon) * gain[:, span] * (g * jax.nn.sigmoid(g))
        normed = normed.astype(BF)
        one, two = dot(normed, mine[span, :], 1, 0), dot(normed, theirs[span, :], 1, 0)
        left = one if left is None else left + one
        right = two if right is None else right + two
    half = mine.shape[1]
    core = core_ref[0]
    out[:, pl.ds(pl.multiple_of(core * half, half), half)] = left.astype(BF)
    out[:, pl.ds(pl.multiple_of((1 - core) * half, half), half)] = right.astype(BF)


pin = lax.optimization_barrier


def swap(a):
    return lax.ppermute(a, "core", [(0, 1), (1, 0)])


def body(
    key_rows,
    value_rows,
    query_rows,
    step_rates,
    fast_gate,
    fast_up,
    fast_down,
    out_gain,
    gate_input,
    out_weight,
):
    chips = lax.axis_size("x")
    place = jnp.stack([lax.axis_index(a).astype(jnp.int32) for a in ("core", "x")])
    tokens, width = key_rows.shape[1:]
    part = fast_gate.shape[1]
    rows = 3 * part
    count = lax.axis_size("hs")
    depth, half = out_weight.shape[0], out_weight.shape[1] // 2
    few = 8
    mine, pieces = pl.pallas_call(
        pack_kernel,
        out_shape=(
            jax.ShapeDtypeStruct((2 * tokens + part, width), BF),
            jax.ShapeDtypeStruct((count, depth, half), BF),
        ),
        in_specs=[SMEM] + [HBM] * 5,
        out_specs=(VMEM, HBM),
        scratch_shapes=[
            pltpu.VMEM((tokens, width), BF),
            pltpu.VMEM((1, tokens), F32),
            pltpu.VMEM((few, depth, half), BF),
            pltpu.SemaphoreType.DMA((5,)),
            pltpu.SemaphoreType.DMA((count // few,)),
        ],
        compiler_params=pltpu.CompilerParams(vmem_limit_bytes=60 * 1024 * 1024),
        name="pack",
    )(place, key_rows[0], value_rows[0], step_rates, fast_down[0], out_weight)
    theirs = swap(mine)
    tail = pl.pallas_call(
        tail_kernel,
        out_shape=jax.ShapeDtypeStruct((part, width), BF),
        in_specs=[VMEM],
        out_specs=VMEM,
        compiler_params=PARAMS,
        name="tail",
    )(theirs)
    pieces, theirs, tail = pin((pieces, theirs, tail))
    left = lax.all_to_all(pieces, "hs", split_axis=0, concat_axis=0, tiled=True).reshape(
        count * depth, half
    )
    weights = pl.pallas_call(
        choose_kernel,
        out_shape=jax.ShapeDtypeStruct((rows + 16, width), BF),
        in_specs=[SMEM] + [VMEM] * 4,
        out_specs=VMEM,
        compiler_params=PARAMS,
        name="choose",
    )(place, fast_gate[0], fast_up[0], fast_down[0], tail)
    held = lax.all_gather(weights, "x", axis=0, tiled=False)
    sums = pl.pallas_call(
        grad_kernel,
        out_shape=(jax.ShapeDtypeStruct((rows, width), BF),) * chips,
        in_specs=[SMEM, VMEM, HBM, VMEM],
        out_specs=(VMEM,) * chips,
        scratch_shapes=[
            pltpu.VMEM((width // 2, width), BF),
            pltpu.VMEM((width // 2, width), BF),
            pltpu.VMEM((width, width // 2), BF),
            pltpu.VMEM((2 * tokens, width), BF),
            pltpu.VMEM((2 * tokens, width), BF),
            pltpu.VMEM((2 * tokens, width // 2), BF),
            pltpu.VMEM((2 * tokens, width // 2), BF),
            pltpu.VMEM((2 * tokens, width // 2), BF),
            pltpu.SemaphoreType.DMA((2, 2)),
        ],
        compiler_params=PARAMS,
        name="grads",
    )(place, mine, theirs, held)
    parts = [
        lax.ppermute(a, "x", [(x, (x + r) % chips) for x in range(chips)]) if r else a
        for r, a in enumerate(sums)
    ]
    new = pl.pallas_call(
        rescale_kernel,
        out_shape=jax.ShapeDtypeStruct((rows, width), BF),
        in_specs=[VMEM] * 5,
        out_specs=VMEM,
        compiler_params=PARAMS,
        name="rescale",
    )(*parts, weights)
    own = lax.all_gather(new, "x", axis=0, tiled=False)
    other = swap(own)
    head_out = pl.pallas_call(
        query_kernel,
        out_shape=jax.ShapeDtypeStruct((tokens, width), BF),
        in_specs=[VMEM] * 4,
        out_specs=VMEM,
        compiler_params=PARAMS,
        name="query",
    )(query_rows[0], held, own, other)
    head_out, left = pin((head_out, left))
    right = swap(left)
    blocks = head_out.reshape(count, tokens // count, width)
    moved = lax.all_to_all(blocks, "hs", split_axis=0, concat_axis=0, tiled=True)
    few, seqs, model = gate_input.shape
    heads = model // width
    columns = out_weight.shape[1]
    result = pl.pallas_call(
        functools.partial(output_kernel, seqs=seqs, heads=heads),
        out_shape=jax.ShapeDtypeStruct((few * seqs, columns), BF),
        in_specs=[SMEM] + [VMEM] * 5,
        out_specs=VMEM,
        compiler_params=PARAMS,
        name="project",
    )(
        place,
        moved.reshape(tokens, width),
        out_gain.reshape(1, model),
        gate_input.reshape(few * seqs, model),
        left,
        right,
    )
    return result.reshape(few, seqs, columns)


def solution(mesh):
    ctx, pairs = mesh.devices.shape
    split = Mesh(mesh.devices.reshape(ctx // 2, 2, pairs), ("x", "core", "hs"))
    c = ("x", "core")
    return jax.shard_map(
        body,
        mesh=split,
        in_specs=(
            P("hs", c, None),
            P("hs", c, None),
            P("hs", c, None),
            P("hs", c),
            P("hs", c, None),
            P("hs", c, None),
            P("hs", c, None),
            P(),
            P(c + ("hs",), None, None),
            P("hs", None),
        ),
        out_specs=P(c + ("hs",), None, None),
        check_vma=False,
    )
```
